32 devices in a mesh: groups: 2 (over y), hid: 4 (over z), wid: 4 (over x, core).
Axes of the slice: x: 2, y: 2, z: 4, core: 2. Of those that a mesh axis runs over, the one named last changes fastest.
Arguments:
- tokens: bfloat16 [1536, 12288], P(('groups', 'hid'), 'wid'), parts along dimension 0, may hold values from -6 to 6
- w_up: bfloat16 [12288, 24576], P('wid', 'hid'), may hold values from -0.0546875 to 0.0546875
- b_up: float32 [24576], P('hid'), may hold values from -4 to 4
- w_down: bfloat16 [24576, 12288], P('hid', 'wid'), may hold values from -0.0390625 to 0.0390625
- b_down: float32 [12288], P('wid'), may hold values from -3 to 3
Outputs:
- mixed: bfloat16 [1536, 12288], P(('groups', 'hid'), 'wid'), parts along dimension 0
The draws below stay inside these ranges and needn't reach their ends.
There are 2 independent parts, one for each index of `groups`. The reference program is written for one: setup_inputs(seed, part) draws one part's arguments, and reference() takes and returns one part's arrays. A program takes and returns all parts, laid end to end along the dimension named above; an argument that names none is the same for every part. Nothing has to cross between parts.
All inputs are finite; a program needn't handle non-finite values.
Results may differ from the reference program's by a relative error of at most 0.0046.
Values may be sent and summed in bfloat16 or wider, within the bound.
A program may use at most 192 MiB of HBM per device.

```python
import jax
import jax.numpy as jnp

D = 12288
FFW = 24576
ROWS = 768


def level_of(rng, dims, cuts, least, largest):
    loudness, own = 1.0, jax.random.fold_in(rng, 6)
    for axis_at, parts in cuts:
        draws = jnp.exp(jax.random.uniform(jax.random.fold_in(own, axis_at), (parts,), jnp.float32, least / len(cuts), largest / len(cuts)))
        loudness = loudness * jnp.repeat(draws, dims[axis_at] // parts).reshape([-1 if axis == axis_at else 1 for axis in range(len(dims))])
    return loudness


def gaussian(stream_key, shape, deviation, most, shards=(), held_as=jnp.bfloat16):
    gain = level_of(stream_key, shape, shards, -0.22, 0.18) if shards else 1.0
    entries = jax.random.normal(stream_key, shape, jnp.float32) * deviation * gain
    return jnp.minimum(jnp.maximum(entries, -most), most).astype(held_as)


def setup_inputs(seed: int = 0, part: int = 0) -> dict:
    arg_keys = jax.random.split(jax.random.key(seed), 6)
    part_keys = jax.random.split(jax.random.fold_in(arg_keys[5], part), 6)
    tokens = gaussian(part_keys[0], (ROWS, D), 1.0, 6.0, ((0, 4), (1, 4)))
    w_up = gaussian(arg_keys[1], (D, FFW), D ** -0.5, 0.0546875, ((0, 4), (1, 4)))
    b_up = gaussian(arg_keys[2], (FFW,), 1.0, 4.0, ((0, 4),), jnp.float32)
    w_down = gaussian(arg_keys[3], (FFW, D), FFW ** -0.5, 0.0390625, ((0, 4), (1, 4)))
    b_down = gaussian(arg_keys[4], (D,), 0.5, 3.0, ((0, 4),), jnp.float32)
    return dict(tokens=tokens, w_up=w_up, b_up=b_up, w_down=w_down, b_down=b_down)


def reference(tokens, w_up, b_up, w_down, b_down):
    pre = jnp.dot(tokens, w_up, preferred_element_type=jnp.float32)
    hidden = jax.nn.gelu(pre + b_up, approximate=True).astype(jnp.bfloat16)
    mixed = jnp.dot(hidden, w_down, preferred_element_type=jnp.float32) + b_down
    return mixed.astype(jnp.bfloat16)
```

```python
import functools

import jax
import jax.numpy as jnp
from jax import lax
from jax.experimental import pallas as pl
from jax.experimental.pallas import tpu as pltpu
from jax.sharding import PartitionSpec as P

CHUNKS = 3
VMEM = 36 * 2**20
F32, BF16 = jnp.float32, jnp.bfloat16


def tile_of(columns, most):
    return max(t for t in range(128, most + 1, 128) if columns % t == 0)


def call(kernel, gates, args, specs, outs, grid, scratch, flops, nbytes):
    def body(*refs):
        kernel(*refs[len(gates):])
    return pl.pallas_call(
        body,
        grid=(grid,),
        in_specs=[pl.BlockSpec(memory_space=pl.ANY)] * len(gates) + specs,
        out_specs=[spec for spec, _ in outs],
        out_shape=[shape for _, shape in outs],
        scratch_shapes=scratch,
        compiler_params=pltpu.CompilerParams(vmem_limit_bytes=VMEM),
        cost_estimate=pl.CostEstimate(flops=flops, bytes_accessed=nbytes, transcendentals=0),
    )(*gates, *args)


def up(slots, w, gates):
    depth, columns = w.shape
    m = sum(s.shape[1] for s in slots)
    tile = tile_of(columns, 512)

    def kernel(*refs):
        slot_refs, (w_ref, own_ref, other_ref, lhs) = refs[:len(slots)], refs[len(slots):]

        @pl.when(pl.program_id(0) == 0)
        def _():
            for h in range(2):
                at = h * m
                for s in slot_refs:
                    lhs[at:at + s.shape[1], :] = s[h]
                    at += s.shape[1]
        pre = jnp.dot(lhs[...], w_ref[...], preferred_element_type=F32)
        own_ref[...] = pre[:m]
        other_ref[...] = pre[m:].astype(BF16)

    specs = [pl.BlockSpec(s.shape, lambda i: (0, 0, 0), pipeline_mode=pl.Buffered(1)) for s in slots]
    specs.append(pl.BlockSpec((depth, tile), lambda i: (0, i)))
    out = pl.BlockSpec((m, tile), lambda i: (0, i))
    return call(
        kernel, gates, [*slots, w], specs,
        [(out, jax.ShapeDtypeStruct((m, columns), F32)), (out, jax.ShapeDtypeStruct((m, columns), BF16))],
        columns // tile, [pltpu.VMEM((2 * m, depth), BF16)],
        4 * m * depth * columns, 2 * depth * columns + 6 * m * columns,
    )


def down(own, other, w, sizes, gates):
    m, depth = own.shape
    columns = w.shape[1]
    tile = tile_of(columns, 256)

    def kernel(own_ref, other_ref, w_ref, *rest):
        outs, lhs = rest[:-1], rest[-1]

        @pl.when(pl.program_id(0) == 0)
        def _():
            lhs[:m, :] = own_ref[...]
            lhs[m:, :] = other_ref[...]
        total = jnp.dot(lhs[...], w_ref[...], preferred_element_type=F32)
        for h in range(2):
            at = h * m
            for o in outs:
                o[h] = total[at:at + o.shape[1]].astype(o.dtype)
                at += o.shape[1]

    lhs_spec = pl.BlockSpec((m, depth), lambda i: (0, 0), pipeline_mode=pl.Buffered(1))
    specs = [lhs_spec, lhs_spec, pl.BlockSpec((depth, tile), lambda i: (0, i))]
    outs = [
        (pl.BlockSpec((2, r, tile), lambda i: (0, 0, i)),
         jax.ShapeDtypeStruct((2, r, columns), BF16 if j else F32))
        for j, r in enumerate(sizes)
    ]
    return call(
        kernel, gates, [own, other, w], specs, outs, columns // tile,
        [pltpu.VMEM((2 * m, depth), BF16)],
        4 * m * depth * columns, 2 * depth * columns + 4 * m * columns,
    )


def pointwise(f, args, bias, gates):
    m, columns = args[0].shape
    tile = tile_of(columns, 1536)
    arrays = list(args) + ([bias.reshape(1, -1)] if bias is not None else [])

    def kernel(*refs):
        refs[-1][...] = f(*[r[...].astype(F32) for r in refs[:-1]]).astype(BF16)

    specs = [pl.BlockSpec((a.shape[0], tile), lambda i: (0, i)) for a in arrays]
    return call(
        kernel, gates, arrays, specs,
        [(pl.BlockSpec((m, tile), lambda i: (0, i)), jax.ShapeDtypeStruct((m, columns), BF16))],
        columns // tile, [], 8 * m * columns, 10 * m * columns,
    )[0]


def activation(*terms):
    return jax.nn.gelu(functools.reduce(jnp.add, terms), approximate=True)


def make(n_hid, n_wid):
    chips = n_wid // 2
    sibling = [(i, i ^ 1) for i in range(n_wid)]

    def per_device(tokens, w_up, b_up, w_down, b_down):
        core = lax.rem(lax.axis_index("wid"), 2)
        rows = tokens.shape[0]
        half = rows // 2
        chunks = CHUNKS if half % CHUNKS == 0 else 1
        step = half // chunks
        apart = step % 16 == 0
        halves = tokens.reshape(2, half, -1)
        halves = jnp.where(core == 0, halves, halves[::-1])

        slots = []
        for k in range(chunks):
            block = halves[:, k * step:(k + 1) * step]
            if k:
                seen = sum(s[0, 0, 0].astype(F32) for s in slots[-1])
                block = jnp.where(jnp.isnan(seen), jnp.zeros_like(block), block)
            got = [block]
            for j in range(1, n_hid):
                got.append(lax.ppermute(block, "hid", [((i + j) % n_hid, i) for i in range(n_hid)]))
            slots.append(got)

        own, other, came, act, outs = {}, {}, {}, {}, {}
        last = []

        def run_up(k):
            nonlocal last
            lhs = slots[k] if apart else [jnp.concatenate(slots[k], axis=1)]
            ahead = [slots[k + 1][0]] if k + 1 < chunks else []
            own[k], mine = up(lhs, w_up, last + ahead)
            last = [mine]
            other[k] = lax.ppermute(mine, "wid", sibling)

        def run_across(k):
            nonlocal last
            send = pointwise(jnp.add, [own[k], other[k]], None, last)
            last = [send]
            came[k] = [
                lax.ppermute(send, "wid", [(i, (i + 2 * d) % n_wid) for i in range(n_wid)])
                for d in range(1, chips)
            ]

        def run_act(k):
            nonlocal last
            mine = pointwise(activation, [own[k], other[k], *came[k]], b_up, last)
            last = [mine]
            act[k] = (mine, lax.ppermute(mine, "wid", sibling))

        def run_down(k):
            nonlocal last
            sizes = [step] * n_hid if apart else [step * n_hid]
            parts = down(*act[k], w_down, sizes, last)
            last = [parts[-1]]
            if not apart:
                whole = parts[0]
                parts = [whole[:, j * step:(j + 1) * step] for j in range(n_hid)]
            total = parts[0]
            for j in range(1, n_hid):
                hops = [(i, (i + j) % n_hid) for i in range(n_hid)]
                total = total + lax.ppermute(parts[j].astype(BF16), "hid", hops).astype(F32)
            outs[k] = (total + b_down).astype(BF16)

        lag = 2
        for t in range(chunks + lag):
            if t < chunks:
                run_up(t)
            if t >= lag:
                run_act(t - lag)
            if t < chunks:
                run_across(t)
            if t >= lag:
                run_down(t - lag)
        out = jnp.concatenate([outs[k] for k in range(chunks)], axis=1)
        return jnp.where(core == 0, out, out[::-1]).reshape(rows, -1)

    return per_device


def solution(mesh):
    return jax.shard_map(
        make(mesh.shape["hid"], mesh.shape["wid"]),
        mesh=mesh,
        in_specs=(
            P(("groups", "hid"), "wid"),
            P("wid", "hid"),
            P("hid"),
            P("hid", "wid"),
            P("wid"),
        ),
        out_specs=P(("groups", "hid"), "wid"),
        check_vma=False,
    )
```

```python
import functools

import jax
import jax.numpy as jnp
from jax import lax
from jax.experimental import pallas as pl
from jax.experimental.pallas import tpu as pltpu
from jax.sharding import PartitionSpec as P

CHUNKS = 3
VMEM = 36 * 2**20
F32, BF16 = jnp.float32, jnp.bfloat16


def tile_of(columns, most):
    return max(t for t in range(128, most + 1, 128) if columns % t == 0)


def call(kernel, gates, args, specs, outs, grid, scratch):
    def body(*refs):
        kernel(*refs[len(gates):])
    return pl.pallas_call(
        body,
        grid=(grid,),
        in_specs=[pl.BlockSpec(memory_space=pl.ANY)] * len(gates) + specs,
        out_specs=[spec for spec, _ in outs],
        out_shape=[shape for _, shape in outs],
        scratch_shapes=scratch,
        compiler_params=pltpu.CompilerParams(vmem_limit_bytes=VMEM),
        cost_estimate=pl.CostEstimate(flops=1024, bytes_accessed=1024, transcendentals=0),
    )(*gates, *args)


def up(slots, w, gates):
    depth, columns = w.shape
    m = sum(s.shape[1] for s in slots)
    tile = tile_of(columns, 512)

    def kernel(*refs):
        slot_refs, (w_ref, own_ref, other_ref, lhs) = refs[:len(slots)], refs[len(slots):]

        @pl.when(pl.program_id(0) == 0)
        def _():
            for h in range(2):
                at = h * m
                for s in slot_refs:
                    lhs[at:at + s.shape[1], :] = s[h]
                    at += s.shape[1]
        pre = jnp.dot(lhs[...], w_ref[...], preferred_element_type=F32)
        own_ref[...] = pre[:m]
        other_ref[...] = pre[m:].astype(BF16)

    specs = [pl.BlockSpec(s.shape, lambda i: (0, 0, 0), pipeline_mode=pl.Buffered(1)) for s in slots]
    specs.append(pl.BlockSpec((depth, tile), lambda i: (0, i)))
    out = pl.BlockSpec((m, tile), lambda i: (0, i))
    return call(
        kernel, gates, [*slots, w], specs,
        [(out, jax.ShapeDtypeStruct((m, columns), F32)), (out, jax.ShapeDtypeStruct((m, columns), BF16))],
        columns // tile, [pltpu.VMEM((2 * m, depth), BF16)],
    )


def down(own, other, w, sizes, gates):
    m, depth = own.shape
    columns = w.shape[1]
    tile = tile_of(columns, 256)

    def kernel(own_ref, other_ref, w_ref, *rest):
        outs, lhs = rest[:-1], rest[-1]

        @pl.when(pl.program_id(0) == 0)
        def _():
            lhs[:m, :] = own_ref[...]
            lhs[m:, :] = other_ref[...]
        total = jnp.dot(lhs[...], w_ref[...], preferred_element_type=F32)
        for h in range(2):
            at = h * m
            for o in outs:
                o[h] = total[at:at + o.shape[1]].astype(o.dtype)
                at += o.shape[1]

    lhs_spec = pl.BlockSpec((m, depth), lambda i: (0, 0), pipeline_mode=pl.Buffered(1))
    specs = [lhs_spec, lhs_spec, pl.BlockSpec((depth, tile), lambda i: (0, i))]
    outs = [
        (pl.BlockSpec((2, r, tile), lambda i: (0, 0, i)),
         jax.ShapeDtypeStruct((2, r, columns), BF16 if j else F32))
        for j, r in enumerate(sizes)
    ]
    return call(
        kernel, gates, [own, other, w], specs, outs, columns // tile,
        [pltpu.VMEM((2 * m, depth), BF16)],
    )


def pointwise(f, args, bias, gates):
    m, columns = args[0].shape
    tile = tile_of(columns, 1536)
    arrays = list(args) + ([bias.reshape(1, -1)] if bias is not None else [])

    def kernel(*refs):
        refs[-1][...] = f(*[r[...].astype(F32) for r in refs[:-1]]).astype(BF16)

    specs = [pl.BlockSpec((a.shape[0], tile), lambda i: (0, i)) for a in arrays]
    return call(
        kernel, gates, arrays, specs,
        [(pl.BlockSpec((m, tile), lambda i: (0, i)), jax.ShapeDtypeStruct((m, columns), BF16))],
        columns // tile, [],
    )[0]


def activation(*terms):
    return jax.nn.gelu(functools.reduce(jnp.add, terms), approximate=True)


def make(n_hid, n_wid):
    chips = n_wid // 2
    sibling = [(i, i ^ 1) for i in range(n_wid)]

    def per_device(tokens, w_up, b_up, w_down, b_down):
        core = lax.rem(lax.axis_index("wid"), 2)
        rows = tokens.shape[0]
        half = rows // 2
        chunks = CHUNKS if half % CHUNKS == 0 else 1
        step = half // chunks
        apart = step % 16 == 0
        halves = tokens.reshape(2, half, -1)
        halves = jnp.where(core == 0, halves, halves[::-1])

        slots = []
        for k in range(chunks):
            block = halves[:, k * step:(k + 1) * step]
            if k:
                seen = sum(s[0, 0, 0].astype(F32) for s in slots[-1])
                block = jnp.where(jnp.isnan(seen), jnp.zeros_like(block), block)
            got = [block]
            for j in range(1, n_hid):
                got.append(lax.ppermute(block, "hid", [((i + j) % n_hid, i) for i in range(n_hid)]))
            slots.append(got)

        own, other, came, act, far, outs = {}, {}, {}, {}, {}, {}
        last = []

        def run_up(k):
            nonlocal last
            lhs = slots[k] if apart else [jnp.concatenate(slots[k], axis=1)]
            ahead = [slots[k + 1][0]] if k + 1 < chunks else []
            own[k], mine = up(lhs, w_up, last + ahead)
            last = [mine]
            other[k] = lax.ppermute(mine, "wid", sibling)

        def run_across(k):
            nonlocal last
            send = pointwise(jnp.add, [own[k], other[k]], None, last)
            last = [send]
            came[k] = [
                lax.ppermute(send, "wid", [(i, (i + 2 * d) % n_wid) for i in range(n_wid)])
                for d in range(1, chips)
            ]

        def run_act(k):
            nonlocal last
            settled = far[k - 2] if k >= 2 else []
            mine = pointwise(activation, [own[k], other[k], *came[k]], b_up, last + settled)
            last = [mine]
            act[k] = (mine, lax.ppermute(mine, "wid", sibling))

        def run_down(k):
            nonlocal last
            sizes = [step] * n_hid if apart else [step * n_hid]
            settled = far[k - 1][:1] if 0 < k == chunks - 1 else []
            parts = down(*act[k], w_down, sizes, last + settled)
            last = [parts[-1]]
            if not apart:
                whole = parts[0]
                parts = [whole[:, j * step:(j + 1) * step] for j in range(n_hid)]
            total = parts[0]
            far[k] = []
            for j in range(1, n_hid):
                hops = [(i, (i + j) % n_hid) for i in range(n_hid)]
                far[k].append(lax.ppermute(parts[j].astype(BF16), "hid", hops))
                total = total + far[k][-1].astype(F32)
            outs[k] = (total + b_down).astype(BF16)

        lag = 1
        for t in range(chunks + lag):
            if t < chunks:
                run_up(t)
            if t >= lag:
                run_act(t - lag)
            if t < chunks:
                run_across(t)
            if t >= lag:
                run_down(t - lag)
        out = jnp.concatenate([outs[k] for k in range(chunks)], axis=1)
        return jnp.where(core == 0, out, out[::-1]).reshape(rows, -1)

    return per_device


def solution(mesh):
    return jax.shard_map(
        make(mesh.shape["hid"], mesh.shape["wid"]),
        mesh=mesh,
        in_specs=(
            P(("groups", "hid"), "wid"),
            P("wid", "hid"),
            P("hid"),
            P("hid", "wid"),
            P("wid"),
        ),
        out_specs=P(("groups", "hid"), "wid"),
        check_vma=False,
    )
```
